32 devices in a mesh: br: 8 (over z, y), bus: 4 (over x, core).
Axes of the slice: x: 2, y: 2, z: 4, core: 2. Of those that a mesh axis runs over, the one named last changes fastest.
Arguments:
- shift_factors: bfloat16 [65536, 8192], P('br', 'bus'), may hold values from -0.09375 to 0.09375
- injections: float32 [8192, 384], P('bus'), may hold values from -6 to 6
- prices: float32 [65536, 384], P(('br', 'bus')), may hold values from -6 to 6
- limits: float32 [65536], P(('br', 'bus')), may hold values from 0.2 to 2
- unit_cost: float32 [8192], P('bus'), may hold values from -1 to 1
- bus_load: float32 [8192], P('bus'), may hold values from 0.5 to 3
- bus_capacity: float32 [8192], P('bus'), may hold values from 0.5 to 3
- irradiance_profile: float32 [64, 256], replicated, may hold values from 0 to 1
- plant_group: int32 [8192], P('bus'), may hold values from 0 to 255
- scenario_profile: int32 [384], replicated, may hold values from 0 to 63
- listed_slab: int32 [256, 3], replicated, may hold values from 0 to 7, all different within a row; in each aligned block of 8 rows (0 to 7, 8 to 15, ...) at most 6 rows name the same one
- listed_block: int32 [256, 3], replicated, may hold values from 0 to 15
- rent_weight: bfloat16 [256, 1536], P(('br', 'bus')), may hold values from -0.15625 to 0.15625
Outputs:
- new_injections: float32 [8192, 384], P('bus')
- new_prices: float32 [65536, 384], P(('br', 'bus'))
- group_rent: float32 [256, 384], P(('br', 'bus'))
The draws below stay inside these ranges and needn't reach their ends.
Inputs may be any that keep to these rules, and one draw needn't show every extreme that they name: `listed_slab`: each plant group names 3 different slabs; among the 8 plant groups of one device (aligned blocks of 8 rows) no slab is named by more than 6 groups, and some device's groups name one slab exactly 6 times.
All inputs are finite; a program needn't handle non-finite values.
Results may differ from the reference program's by a relative error of at most 0.0052.
Values may be sent and summed in bfloat16 or wider, within the bound.
A program may use at most 128 MiB of HBM per device.

```python
import math
import jax
import jax.numpy as jnp
import numpy as np
from jax import lax

BRANCHES = 65536
BUSES = 8192
SCEN = 384
BLOCK = 512
LISTS = 3
CAP = 6
GDEV = 8
PROFILES = 64
SLAB = 8192
GROUPS = 256
N_BR = 8


def set_ends(drawn, rng, least, high):
    longest = drawn.shape.index(max(drawn.shape))
    spots = []
    for shift in (0, 1):
        where = [jax.random.randint(jax.random.fold_in(rng, axis), (), 0, length) for axis, length in enumerate(drawn.shape)]
        where[longest] = (where[longest] + shift) % drawn.shape[longest]
        spots.append(tuple(where))
    return drawn.at[spots[0]].set(least).at[spots[1]].set(high)


def raised(drawn, rng, source, target, blocks, factor):
    def block_of(dim):
        return (jnp.arange(drawn.shape[dim]) // (drawn.shape[dim] // blocks)).reshape((-1,) + (1,) * (drawn.ndim - 1 - dim))

    near = jax.random.permutation(rng, blocks)[block_of(target)]
    far = (block_of(target) + blocks // 2) % blocks
    return jnp.where((block_of(source) == near) | (block_of(source) == far), factor * drawn, drawn)


def block_levels(key, extent, split, least, high):
    gain, own = 1.0, jax.random.fold_in(key, 6)
    for axis_at, parts in split:
        steps = jnp.exp(jax.random.uniform(jax.random.fold_in(own, axis_at), (parts,), jnp.float32, least / len(split), high / len(split)))
        gain = gain * jnp.repeat(steps, extent[axis_at] // parts).reshape([-1 if axis == axis_at else 1 for axis in range(len(extent))])
    return gain


def assign_block(key, own, number, rows, number_of, top, most, skew):
    order = jax.random.permutation(key, number_of)
    packed, ordinary = shares(number_of, rows * top, most, skew, True), shares(number_of, rows * top, most, skew, False)
    places = jnp.arange(number_of)

    def named(tallies, turn):
        used = int((tallies > 0).sum())
        fixed = max(1, used // 4)
        shifted = fixed + (places - fixed + turn * (used - fixed)) % max(1, number_of - fixed)
        return jnp.zeros((number_of,), jnp.int32).at[order[jnp.where(places < fixed, places, shifted)]].set(jnp.asarray(tallies, jnp.int32))

    tallies = jnp.where(number % 4 == 0, named(packed, number // 4), named(ordinary, number - number // 4 - 1))
    mixed = jax.random.permutation(jax.random.fold_in(own, 3), number_of)
    donor, receiver = mixed[0:number_of // 2 * 2:2], mixed[1:number_of // 2 * 2:2]
    room = jnp.minimum(tallies[donor] - 1, most - tallies[receiver]) // 2
    room = jnp.where((donor == order[0]) | (receiver == order[0]) | (tallies[receiver] == 0), 0, jnp.maximum(room, 0))
    shifted = jax.random.randint(jax.random.fold_in(own, 4), (number_of // 2,), 0, 1 << 20) % (room + 1)
    tallies = tallies.at[donor].add(-shifted).at[receiver].add(shifted)
    labels = jnp.searchsorted(jnp.cumsum(tallies), jnp.arange(rows * top), side="right").astype(jnp.int32)
    listing = labels.reshape(top, rows).T
    listing = listing[jax.random.permutation(jax.random.fold_in(own, 1), rows)]
    turn = jax.random.randint(jax.random.fold_in(own, 2), (rows, 1), 0, top)
    return jnp.take_along_axis(listing, (jnp.arange(top)[None, :] + turn) % top, axis=1)


def shares(count, total, most, slope, full):
    weights = [(1 << 20) // math.isqrt(grade ** slope) + 1 for grade in range(1, count + 1)]
    largest = most if full else min(most, max(-(-total // count), total * weights[0] // sum(weights)))
    least = 1 if total - largest >= count - 1 else 0
    holding, surplus = [largest] + [least] * (count - 1), total - largest - least * (count - 1)
    while surplus > 0:
        candidates = [i for i in range(1, count) if holding[i] < largest] or [i for i in range(1, count) if holding[i] < most]
        pool, left = sum([weights[i] for i in candidates]), surplus
        for i in candidates:
            more = min(most - holding[i], max(1, left * weights[i] // pool), surplus)
            holding[i] = holding[i] + more
            surplus = surplus - more
    return np.array(holding)


def gaussian(stream_key, dims, scale, reach, pieces=(), held_as=jnp.bfloat16):
    level = block_levels(stream_key, dims, pieces, -0.22, 0.18) if pieces else 1.0
    result = jax.random.normal(stream_key, dims, jnp.float32) * scale * level
    return jnp.minimum(jnp.maximum(result, -reach), reach).astype(held_as)


def bell_draw_with(own_key, extent, width, most, split, heavy, dtype=jnp.bfloat16):
    array = width * jax.random.normal(own_key, extent, jnp.float32)
    if split:
        array = array * block_levels(own_key, extent, split, -0.22, 0.18)
    return jnp.clip(raised(array, jax.random.fold_in(own_key, 3), *heavy), -most, most).astype(dtype)


def setup_inputs(seed: int = 0) -> dict:
    streams_of = jax.random.split(jax.random.key(seed), 14)
    shift_factors = bell_draw_with(streams_of[0], (BRANCHES, BUSES), BUSES ** -0.5, 0.09375, ((0, 8), (1, 4)), (1, 0, 8, 2.0))
    injections = gaussian(streams_of[1], (BUSES, SCEN), 1.0, 6.0, ((0, 4),), jnp.float32)
    prices = gaussian(streams_of[2], (BRANCHES, SCEN), 1.0, 6.0, ((0, 32),), jnp.float32)
    limits = jnp.clip(jnp.exp(math.log(2.0) - 2.3025851 * jax.random.uniform(streams_of[3], (BRANCHES,), jnp.float32) ** block_levels(streams_of[3], (BRANCHES,), ((0, 32),), -0.2, 0.2)), 0.2, 2.0)
    unit_cost = jnp.clip(jax.random.uniform(streams_of[4], (BUSES,), jnp.float32, -1.0, 1.0) * block_levels(streams_of[4], (BUSES,), ((0, 4),), -0.4, 0.0), -1.0, 1.0)
    bus_load = jnp.clip(jnp.exp(math.log(3.0) - 1.7917595 * jax.random.uniform(streams_of[5], (BUSES,), jnp.float32) ** block_levels(streams_of[5], (BUSES,), ((0, 4),), -0.2, 0.2)), 0.5, 3.0)
    bus_capacity = jnp.clip(jnp.exp(math.log(3.0) - 1.7917595 * jax.random.uniform(streams_of[6], (BUSES,), jnp.float32) ** block_levels(streams_of[6], (BUSES,), ((0, 4),), -0.2, 0.2)), 0.5, 3.0)
    irradiance_profile = jnp.clip(jax.random.uniform(streams_of[7], (PROFILES, GROUPS), jnp.float32, 0.0, 1.0), 0.0, 1.0)
    plant_group = set_ends(jax.random.randint(streams_of[8], (BUSES,), 0, GROUPS), jax.random.fold_in(streams_of[8], 1), 0, GROUPS - 1).astype(jnp.int32)
    scenario_profile = set_ends(jax.random.randint(streams_of[9], (SCEN,), 0, PROFILES), jax.random.fold_in(streams_of[9], 1), 0, PROFILES - 1).astype(jnp.int32)
    listed_slab_keys = jax.random.split(jax.random.fold_in(streams_of[10], 1), GROUPS // GDEV)
    listed_slab_turns = jax.random.permutation(jax.random.fold_in(streams_of[10], 3), GROUPS // GDEV)
    listed_slab = jax.vmap(lambda own, number: assign_block(jax.random.fold_in(streams_of[10], 2), own, number, GDEV, N_BR, LISTS, CAP, 2))(listed_slab_keys, listed_slab_turns).reshape((GROUPS, LISTS))
    listed_block = set_ends(jax.random.randint(streams_of[11], (GROUPS, LISTS), 0, SLAB // BLOCK), jax.random.fold_in(streams_of[11], 1), 0, (SLAB // BLOCK) - 1).astype(jnp.int32)
    rent_weight = gaussian(streams_of[12], (GROUPS, LISTS * BLOCK), (LISTS * BLOCK) ** -0.5, 0.15625, ((0, 32),))
    return dict(shift_factors=shift_factors, injections=injections, prices=prices, limits=limits, unit_cost=unit_cost, bus_load=bus_load, bus_capacity=bus_capacity, irradiance_profile=irradiance_profile, plant_group=plant_group, scenario_profile=scenario_profile, listed_slab=listed_slab, listed_block=listed_block, rent_weight=rent_weight)


step_dual = 0.5
step_primal = 0.25


def reference(shift_factors, injections, prices, limits, unit_cost, bus_load, bus_capacity, irradiance_profile, plant_group, scenario_profile, listed_slab, listed_block, rent_weight):
    inject_half = injections.astype(jnp.bfloat16)
    flow = jnp.dot(shift_factors, inject_half, preferred_element_type=jnp.float32)
    moved = prices + step_dual * flow
    bound = step_dual * limits[:, None]
    new_prices = moved - jnp.clip(moved, -bound, bound)
    price_half = new_prices.astype(jnp.bfloat16)
    gradient = jnp.dot(shift_factors.T, price_half, preferred_element_type=jnp.float32)
    share = irradiance_profile[scenario_profile][:, plant_group].T
    upper = bus_capacity[:, None] * share
    trial = injections - step_primal * (unit_cost[:, None] + gradient)
    new_injections = jnp.minimum(jnp.maximum(trial, -bus_load[:, None]), upper)
    blocks = price_half.reshape(BRANCHES // BLOCK, BLOCK, SCEN)
    block_ids = (listed_slab * (SLAB // BLOCK) + listed_block).astype(jnp.int32)
    weights = rent_weight.reshape(GROUPS, LISTS, BLOCK)

    def one_group(item):
        weight_rows, ids = item
        picked = jnp.take(blocks, ids, axis=0).astype(jnp.float32)
        return jnp.einsum("kr,krs->s", weight_rows.astype(jnp.float32), picked)

    group_rent = lax.map(one_group, (weights, block_ids))
    return new_injections, new_prices, group_rent
```

```python
import jax
import jax.numpy as jnp
from jax import lax
from jax.sharding import PartitionSpec as P

BLOCK = 512
GDEV = 8


step_dual = 0.5
step_primal = 0.25


def partners(size, bit):
    return [(i, i ^ (1 << bit)) for i in range(size)]


def halving_sum(x, axis, order, wide=()):
    size = x.shape[0]
    levels = size.bit_length() - 1
    me = lax.axis_index(axis)
    rows, width = x.shape[1:]
    x = x.reshape((2,) * levels + (rows, width))
    for bit in order:
        dim = levels - 1 - bit
        mine = (me >> bit) & 1
        keep = lax.dynamic_index_in_dim(x, mine, dim)
        send = lax.dynamic_index_in_dim(x, 1 - mine, dim)
        if bit not in wide:
            send = send.astype(jnp.bfloat16)
        x = keep + lax.ppermute(send, axis, partners(size, bit)).astype(jnp.float32)
    return x.reshape(rows, width)


def doubling_gather(x, axis, order):
    size = lax.axis_size(axis)
    levels = size.bit_length() - 1
    me = lax.axis_index(axis)
    rows, width = x.shape
    x = x.reshape((1,) * levels + (rows, width))
    for bit in reversed(order):
        dim = levels - 1 - bit
        upper = ((me >> bit) & 1) == 1
        other = lax.ppermute(x, axis, partners(size, bit))
        x = jnp.concatenate([jnp.where(upper, other, x), jnp.where(upper, x, other)], axis=dim)
    return x.reshape(size, rows, width)


def per_device(
    shift_factors,
    injections,
    prices,
    limits,
    unit_cost,
    bus_load,
    bus_capacity,
    irradiance_profile,
    plant_group,
    scenario_profile,
    listed_slab,
    listed_block,
    rent_weight,
):
    bus_axis = lax.axis_size("bus")
    slab_axis = lax.axis_size("br")
    slab_index = lax.axis_index("br")
    column_index = lax.axis_index("bus")
    weights = lax.all_gather(rent_weight, "br", axis=0, tiled=True)
    list_len = listed_slab.shape[1]
    groups = weights.shape[0]
    per_slab = shift_factors.shape[0] // BLOCK
    lists = jnp.stack([listed_slab, listed_block], axis=-1)
    lists = lists.reshape(slab_axis, bus_axis, GDEV, list_len, 2)
    lists = lax.dynamic_index_in_dim(lists, column_index, 1, keepdims=False)
    lists = lists.reshape(groups, list_len, 2)
    here = (lists[..., 0] == slab_index)[:, :, None] & (
        lists[..., 1][:, :, None] == jnp.arange(per_slab, dtype=jnp.int32)
    )
    weights = weights.reshape(groups, list_len, BLOCK)
    spread = jnp.zeros((groups, per_slab, BLOCK), weights.dtype)
    for k in range(list_len):
        spread = jnp.where(here[:, k, :, None], weights[:, k, None, :], spread)
    spread = spread.reshape(groups, per_slab * BLOCK)

    inject_half = injections.astype(jnp.bfloat16)
    bound = step_dual * limits[:, None]
    scenarios = injections.shape[1]
    cut = max(128, scenarios // 128 * 2 // 3 * 128)
    bus_order = tuple(range(bus_axis.bit_length() - 1))
    br_order = tuple(range(slab_axis.bit_length() - 1))
    parts = ((0, cut), (cut, scenarios))
    buses = shift_factors.shape[1]
    flows = [
        jnp.dot(shift_factors, inject_half[:, lo:hi], preferred_element_type=jnp.float32)
        for lo, hi in parts
    ]
    new_parts, grad_parts, rent_parts = [], [], []
    for (lo, hi), partial_flow in zip(parts, flows):
        width = hi - lo
        flow = halving_sum(partial_flow.reshape(bus_axis, -1, width), "bus", bus_order, (0,))
        moved = prices[:, lo:hi] + step_dual * flow
        new_part = moved - jnp.clip(moved, -bound, bound)
        new_parts.append(new_part)
        slab_prices = doubling_gather(new_part.astype(jnp.bfloat16), "bus", bus_order)
        slab_prices = slab_prices.reshape(-1, width)
        partial_grad = lax.dot_general(
            shift_factors, slab_prices, (((0,), (0,)), ((), ())), preferred_element_type=jnp.float32
        )
        partial_rent = jnp.dot(spread, slab_prices, preferred_element_type=jnp.float32)
        half = buses // 2
        first = jnp.concatenate(
            [
                partial_grad[:half].reshape(slab_axis, -1, width),
                partial_rent.reshape(slab_axis, GDEV, width),
            ],
            axis=1,
        )
        second = partial_grad[half:].reshape(slab_axis, -1, width)
        first = halving_sum(first, "br", br_order)
        second_order = br_order[1:] + br_order[:1]
        second = halving_sum(second, "br", second_order)
        rent_parts.append(first[half // slab_axis:])
        first = doubling_gather(first[:half // slab_axis].astype(jnp.bfloat16), "br", br_order)
        second = doubling_gather(second.astype(jnp.bfloat16), "br", second_order)
        grad_parts.append(
            jnp.concatenate([first.reshape(half, width), second.reshape(half, width)], axis=0)
        )
    new_prices = jnp.concatenate(new_parts, axis=1)
    gradient = jnp.concatenate(grad_parts, axis=1).astype(jnp.float32)
    group_rent = jnp.concatenate(rent_parts, axis=1)
    group_count = irradiance_profile.shape[1]
    profile_count = irradiance_profile.shape[0]
    pick_group = (plant_group[:, None] == jnp.arange(group_count, dtype=jnp.int32)[None, :]).astype(
        jnp.float32
    )
    bus_profile = jnp.dot(pick_group, irradiance_profile.T, precision=lax.Precision.HIGHEST)
    pick_scenario = (
        jnp.arange(profile_count, dtype=jnp.int32)[:, None] == scenario_profile[None, :]
    ).astype(jnp.float32)
    share = jnp.dot(bus_profile, pick_scenario, precision=lax.Precision.HIGHEST)
    upper = bus_capacity[:, None] * share
    trial = injections - step_primal * (unit_cost[:, None] + gradient)
    new_injections = jnp.minimum(jnp.maximum(trial, -bus_load[:, None]), upper)
    return (new_injections, new_prices, group_rent)


def solution(mesh):
    placed = (
        P("br", "bus"),
        P("bus", None),
        P(("br", "bus"), None),
        P(("br", "bus")),
        P("bus"),
        P("bus"),
        P("bus"),
        P(),
        P("bus"),
        P(),
        P(),
        P(),
        P(("br", "bus"), None),
    )
    return jax.shard_map(
        per_device,
        mesh=mesh,
        in_specs=placed,
        out_specs=(P("bus", None), P(("br", "bus"), None), P(("br", "bus"), None)),
        check_vma=False,
    )
```
